32 devices in a mesh: set: 1, kb: 32 (over z, y, x, core).
Axes of the slice: x: 2, y: 2, z: 4, core: 2. Of those that a mesh axis runs over, the one named last changes fastest.
Arguments:
- green_momentum_grid: float32 [2, 4, 4096, 512], P('set', None, 'kb'), may hold values from -6 to 6
- pair_table: int32 [8, 2], replicated, may hold values from 0 to 3, as said below
- mirror_map: int32 [3, 16], P('set'), may hold values from 0 to 15, as said below
Outputs:
- chi_out: float32 [2, 8, 4096, 512], P('set', None, 'kb')
The draws below stay inside these ranges and needn't reach their ends.
Inputs may be any that keep to these rules, and one draw needn't show every extreme that they name: `pair_table`: each of the two columns names every entry number 0 to 3 at least once. Each row d is a reflection: mirror_map[d,x] = (c_d - x) mod 16 for a centre c_d of that row.
All inputs are finite; a program needn't handle non-finite values.
Results may differ from the reference program's by a relative error of at most 0.0003.
Values sent between devices are 32-bit elements; how exact they have to be, the bound alone decides.
A program may use at most 128 MiB of HBM per device.

```python
import math
import jax
import jax.numpy as jnp
from jax import lax

SIDE = 16
KPTS = 4096
NFREQ = 512
NENT = 4
NCHI = 8


def draw_pair_table(key, part):
    column_one = jax.random.permutation(jax.random.fold_in(key, 11), jnp.arange(NCHI, dtype=jnp.int32) % NENT)
    column_two = jax.random.permutation(jax.random.fold_in(key, 12), jnp.arange(NCHI, dtype=jnp.int32) % NENT)
    return jnp.stack([column_one, column_two], axis=1).astype(jnp.int32)


def draw_mirror_map(key, part):
    centres = jax.random.randint(jax.random.fold_in(key, 21), (3,), 0, SIDE, dtype=jnp.int32)
    coords = jnp.arange(SIDE, dtype=jnp.int32)
    return ((centres[:, None] - coords[None, :]) % SIDE).astype(jnp.int32)


def steps_of(stream_key, shape, pieces, least, high):
    gain = 1.0
    for dim, shards_of in pieces:
        steps = jax.random.uniform(jax.random.fold_in(jax.random.fold_in(stream_key, 6), dim), (shards_of,), jnp.float32, least / len(pieces), high / len(pieces))
        gain = gain * jnp.repeat(jnp.exp(steps), shape[dim] // shards_of).reshape((-1,) + (1,) * (len(shape) - 1 - dim))
    return gain


def gaussian(rng, shape, width, limit, cuts=(), kind=jnp.bfloat16):
    result = jax.random.normal(rng, shape, jnp.float32) * width
    if len(cuts) > 0:
        result = steps_of(rng, shape, cuts, -0.22, 0.18) * result
    return jnp.clip(result, min=-limit, max=limit).astype(kind)


def setup_inputs(seed: int = 0, part: int = 0) -> dict:
    key_of = jax.random.split(jax.random.key(seed), 4)
    own_keys = jax.random.split(jax.random.fold_in(key_of[3], part), 4)
    green_momentum_grid = gaussian(own_keys[0], (2, NENT, KPTS, NFREQ), 1.0, 6.0, ((2, 32),), jnp.float32)
    pair_table = draw_pair_table(jax.random.fold_in(key_of[3], 71), part)
    mirror_map = draw_mirror_map(jax.random.fold_in(jax.random.fold_in(key_of[3], part), 71), part)
    return {"green_momentum_grid": green_momentum_grid, "pair_table": pair_table, "mirror_map": mirror_map}


def trig_pair(angle_int, period, scale):
    angle = (2.0 * math.pi / period) * angle_int.astype(jnp.float32)
    return scale * jnp.cos(angle), scale * jnp.sin(angle)


def complex_combine(formula, cosine, sine, real_part, imag_part):
    first_term = jnp.einsum(formula, cosine, real_part + imag_part, precision=lax.Precision.HIGHEST)
    second_term = jnp.einsum(formula, cosine + sine, imag_part, precision=lax.Precision.HIGHEST)
    third_term = jnp.einsum(formula, sine - cosine, real_part, precision=lax.Precision.HIGHEST)
    return first_term - second_term, first_term + third_term


def forward_imaginary_time(tau_rows, frequency_count):
    freq_index = jnp.arange(frequency_count, dtype=jnp.int32)
    angle_int = ((2 * freq_index[None, :] - frequency_count + 1) * (2 * tau_rows[:, None] + 1)) % (4 * frequency_count)
    cosine, sine = trig_pair(angle_int, 4 * frequency_count, frequency_count ** -0.5)
    return cosine, -sine


def tau_backward(tau_rows, frequency_count):
    freq_index = jnp.arange(frequency_count, dtype=jnp.int32)
    angle_int = ((freq_index[:, None] - frequency_count // 2) * (2 * tau_rows[None, :] + 1)) % (2 * frequency_count)
    return trig_pair(angle_int, 2 * frequency_count, frequency_count ** -0.5)


def grid_transform(real_part, imag_part, grid_side, direction):
    shape = real_part.shape
    plane = jnp.arange(grid_side * grid_side, dtype=jnp.int32)
    upper = plane // grid_side
    lower = plane % grid_side
    plane_int = (upper[:, None] * upper[None, :] + lower[:, None] * lower[None, :]) % grid_side
    plane_cos, plane_sin = trig_pair(plane_int, grid_side, 1.0 / grid_side)
    line = jnp.arange(grid_side, dtype=jnp.int32)
    line_cos, line_sin = trig_pair((line[:, None] * line[None, :]) % grid_side, grid_side, grid_side ** -0.5)
    real_part = real_part.reshape(shape[:-1] + (grid_side, grid_side * grid_side))
    imag_part = imag_part.reshape(shape[:-1] + (grid_side, grid_side * grid_side))
    real_part, imag_part = complex_combine('pq,...xq->...xp', plane_cos, direction * plane_sin, real_part, imag_part)
    real_part, imag_part = complex_combine('ax,...xp->...ap', line_cos, direction * line_sin, real_part, imag_part)
    return real_part.reshape(shape), imag_part.reshape(shape)


def mirror_index(mirror_map, grid_side):
    index_x = mirror_map[0][:, None, None]
    index_y = mirror_map[1][None, :, None]
    index_z = mirror_map[2][None, None, :]
    return (index_x * grid_side * grid_side + index_y * grid_side + index_z).reshape(-1).astype(jnp.int32)


def bubble(gr_re, gr_im, mirror_re, mirror_im, pair_table, entries):
    entry_ids = jnp.arange(entries, dtype=jnp.int32)
    pick_left = (pair_table[:, 0][:, None] == entry_ids[None, :]).astype(jnp.float32)
    pick_right = (pair_table[:, 1][:, None] == entry_ids[None, :]).astype(jnp.float32)
    left_re = jnp.einsum('me,e...->m...', pick_left, gr_re, precision=lax.Precision.HIGHEST)
    left_im = jnp.einsum('me,e...->m...', pick_left, gr_im, precision=lax.Precision.HIGHEST)
    right_re = jnp.einsum('me,e...->m...', pick_right, mirror_re, precision=lax.Precision.HIGHEST)
    right_im = jnp.einsum('me,e...->m...', pick_right, mirror_im, precision=lax.Precision.HIGHEST)
    return left_re * right_re - left_im * right_im, left_re * right_im + left_im * right_re


def reference(green_momentum_grid, pair_table, mirror_map):
    tau_rows = jnp.arange(NFREQ, dtype=jnp.int32)
    fwd_cos, fwd_sin = forward_imaginary_time(tau_rows, NFREQ)
    tau_re, tau_im = complex_combine('qa,fsa->fqs', fwd_cos, fwd_sin, green_momentum_grid[0], green_momentum_grid[1])
    mirror_flat = mirror_index(mirror_map, SIDE)

    def one_time(time_index):
        other_index = (NFREQ - 1 - time_index).astype(jnp.int32)
        here_re = lax.dynamic_index_in_dim(tau_re, time_index, 1, keepdims=False)
        here_im = lax.dynamic_index_in_dim(tau_im, time_index, 1, keepdims=False)
        there_re = lax.dynamic_index_in_dim(tau_re, other_index, 1, keepdims=False)
        there_im = lax.dynamic_index_in_dim(tau_im, other_index, 1, keepdims=False)
        here_re, here_im = grid_transform(here_re, here_im, SIDE, 1.0)
        there_re, there_im = grid_transform(there_re, there_im, SIDE, 1.0)
        there_re = jnp.take(there_re, mirror_flat, axis=1)
        there_im = jnp.take(there_im, mirror_flat, axis=1)
        chi_re, chi_im = bubble(here_re, here_im, there_re, there_im, pair_table, NENT)
        chi_re, chi_im = grid_transform(chi_re, chi_im, SIDE, -1.0)
        return jnp.stack([chi_re, chi_im])

    momenta = lax.map(one_time, jnp.arange(NFREQ, dtype=jnp.int32))
    momenta = jnp.transpose(momenta, (1, 2, 0, 3))
    back_cos, back_sin = tau_backward(tau_rows, NFREQ)
    out_re, out_im = complex_combine('vj,ejk->ekv', back_cos, back_sin, momenta[0], momenta[1])
    return jnp.stack([out_re, out_im])
```

```python
import functools

import numpy as np
import ml_dtypes
import jax
import jax.numpy as jnp
from jax import lax
from jax.experimental import pallas as pl
from jax.experimental.pallas import tpu as pltpu
from jax.sharding import PartitionSpec as P

CHUNKS = 2
VMEM = pl.BlockSpec(memory_space=pltpu.VMEM)
SMEM = pl.BlockSpec(memory_space=pltpu.SMEM)
PARAMS = pltpu.CompilerParams(vmem_limit_bytes=48 * 1024 * 1024)


def split_np(table):
    table = table.astype(np.float32)
    high = table.astype(ml_dtypes.bfloat16)
    low = (table - high.astype(np.float32)).astype(ml_dtypes.bfloat16)
    return high, low


def split(x):
    high = x.astype(jnp.bfloat16)
    return high, (x - high.astype(jnp.float32)).astype(jnp.bfloat16)


def mm(a, b, dims):
    return lax.dot_general(a, b, (dims, ((), ())), preferred_element_type=jnp.float32)


def mm3(a, b, dims=((1,), (0,))):
    return mm(a[0], b[0], dims) + mm(a[1], b[0], dims) + mm(a[0], b[1], dims)


def owned_times(devices, freqs, chunk):
    per = freqs // (2 * CHUNKS * devices)
    first = chunk * (freqs // (2 * CHUNKS)) + np.arange(devices)[:, None] * per + np.arange(per)[None, :]
    return np.stack([first, freqs - 1 - first], axis=1).reshape(-1)


def time_tables(times, freqs):
    angle = ((2 * np.arange(freqs)[None, :] - freqs + 1) * (2 * times[:, None] + 1)) % (4 * freqs)
    angle = angle * (2 * np.pi / (4 * freqs))
    scale = freqs**-0.5
    return split_np(scale * np.cos(angle)) + split_np(scale * np.sin(angle))


def frequency_tables(times, freqs):
    angle = ((np.arange(freqs)[None, :] - freqs // 2) * (2 * times[:, None] + 1)) % (2 * freqs)
    angle = angle * (2 * np.pi / (2 * freqs))
    cos, sin = np.cos(angle) * freqs**-0.5, np.sin(angle) * freqs**-0.5
    return split_np(np.block([[cos, sin], [-sin, cos]]))


def plane_table(side, sign):
    index = np.arange(side * side)
    upper, lower = index // side, index % side
    angle = (upper[:, None] * upper[None, :] + lower[:, None] * lower[None, :]) % side * (2 * np.pi / side)
    scale = (side**3) ** -0.5
    cos, sin = scale * np.cos(angle), sign * scale * np.sin(angle)
    return split_np(np.block([[cos, sin], [-sin, cos]]))


def cadd(a, b):
    return a[0] + b[0], a[1] + b[1]


def csub(a, b):
    return a[0] - b[0], a[1] - b[1]


def dft4(a, sign):
    s02, d02 = cadd(a[0], a[2]), csub(a[0], a[2])
    s13, d13 = cadd(a[1], a[3]), csub(a[1], a[3])
    turned = (-d13[1], d13[0]) if sign > 0 else (d13[1], -d13[0])
    return [cadd(s02, s13), cadd(d02, turned), csub(s02, s13), csub(d02, turned)]


def twiddle(a, power, sign):
    if power == 0:
        return a
    if power == 4:
        return (-a[1], a[0]) if sign > 0 else (a[1], -a[0])
    if power in (2, 6):
        r = np.float32(np.sqrt(0.5))
        plus, minus = (a[0] + a[1]) * r, (a[0] - a[1]) * r
        if power == 2:
            return (minus, plus) if sign > 0 else (plus, -minus)
        return (-plus, minus) if sign > 0 else (-minus, -plus)
    c = np.float32(np.cos(2 * np.pi * power / 16))
    s = np.float32(sign * np.sin(2 * np.pi * power / 16))
    return a[0] * c - a[1] * s, a[0] * s + a[1] * c


def dft16(x, sign):
    columns = [dft4([x[4 * n1 + n2] for n1 in range(4)], sign) for n2 in range(4)]
    out = [None] * 16
    for k1 in range(4):
        row = dft4([twiddle(columns[n2][k1], n2 * k1, sign) for n2 in range(4)], sign)
        for k2 in range(4):
            out[k1 + 4 * k2] = row[k2]
    return out


def to_time_kernel(g_ref, ch_ref, cl_ref, sh_ref, sl_ref, o_ref):
    devices, _, entries, slots, points = o_ref.shape
    freqs = g_ref.shape[-1]
    cos, sin = (ch_ref[...], cl_ref[...]), (sh_ref[...], sl_ref[...])
    dims = ((1,), (1,))
    re = split(g_ref[0].reshape(entries * points, freqs))
    im = split(g_ref[1].reshape(entries * points, freqs))
    tau = (mm3(cos, re, dims) + mm3(sin, im, dims), mm3(cos, im, dims) - mm3(sin, re, dims))
    for part in range(2):
        for e in range(entries):
            o_ref[:, part, e] = tau[part][:, e * points:(e + 1) * points].reshape(devices, slots, points)


def bubble_kernel(pair_ref, mirror_ref, x_ref, wh_ref, wl_ref, mh_ref, ml_ref, ih_ref, il_ref, o_ref, y, g, gm, chi):
    devices, _, entries, slots, points = x_ref.shape
    side = y.shape[0]
    plane = side * side
    halves = devices // side
    comps = o_ref.shape[2]
    for h in range(halves):
        for e in range(entries):
            cells = [(x_ref[k * halves + h, 0, e], x_ref[k * halves + h, 1, e]) for k in range(side)]
            for k, (re, im) in enumerate(dft16(cells, 1)):
                y[k, e, :, h * points:(h + 1) * points] = re
                y[k, e, :, plane + h * points:plane + (h + 1) * points] = im
    rows = split(y[...].reshape(side * entries * slots, 2 * plane))
    g[...] = mm3(rows, (wh_ref[...], wl_ref[...])).reshape(g.shape)
    other = mm3(rows, (mh_ref[...], ml_ref[...])).reshape(side * entries, slots, 2 * plane)
    other = jnp.concatenate([other[:, slots // 2:], other[:, :slots // 2]], axis=1)
    gm[...] = other.reshape(gm.shape)

    def one(c, carry):
        left, right = pair_ref[c, 0], pair_ref[c, 1]
        for r in range(side):
            a = g[r, left]
            b = gm[mirror_ref[0, r], right]
            ar, ai, br, bi = a[:, :plane], a[:, plane:], b[:, :plane], b[:, plane:]
            chi[c, r, :, :plane] = ar * br - ai * bi
            chi[c, r, :, plane:] = ar * bi + ai * br
        return carry

    lax.fori_loop(0, comps, one, 0)
    rows = split(chi[...].reshape(comps * side * slots, 2 * plane))
    chi[...] = mm3(rows, (ih_ref[...], il_ref[...])).reshape(chi.shape)

    def back(c, carry):
        for h in range(halves):
            lanes = slice(h * points, (h + 1) * points)
            high = slice(plane + h * points, plane + (h + 1) * points)
            cells = [(chi[c, r, :, lanes], chi[c, r, :, high]) for r in range(side)]
            for q, (re, im) in enumerate(dft16(cells, -1)):
                o_ref[q * halves + h, 0, c] = re
                o_ref[q * halves + h, 1, c] = im
        return carry

    lax.fori_loop(0, comps, back, 0)


def to_frequency_kernel(first, *refs):
    x_ref, bh_ref, bl_ref = refs[:3]
    o_ref = refs[-1]
    devices, _, block, slots, points = x_ref.shape
    freqs = o_ref.shape[-1]
    rows = []
    for c in range(block):
        parts = [x_ref[:, part, c].reshape(devices * slots, points).T for part in range(2)]
        rows.append(jnp.concatenate(parts, axis=1))
    value = mm3(split(jnp.concatenate(rows, axis=0)), (bh_ref[...], bl_ref[...]))
    for part in range(2):
        lanes = value[:, part * freqs:(part + 1) * freqs].reshape(block, points, freqs)
        o_ref[part] = lanes if first else refs[3][part] + lanes


def local(devices, green, pair_table, mirror_map):
    entries, points, freqs = green.shape[1:]
    side = mirror_map.shape[1]
    plane = side * side
    comps = pair_table.shape[0]
    slots = freqs // (devices * CHUNKS)
    f32 = jnp.float32
    ahead = plane_table(side, 1.0)
    inverse = plane_table(side, -1.0)
    target = (mirror_map[1][:, None] * side + mirror_map[2][None, :]).reshape(1, plane)
    pick = (lax.broadcasted_iota(jnp.int32, (plane, plane), 0) == target).astype(jnp.bfloat16)
    mirrored = [
        jnp.einsum("apk,kr->apr", t.reshape(2 * plane, 2, plane), pick, preferred_element_type=jnp.bfloat16)
        .reshape(2 * plane, 2 * plane)
        for t in ahead
    ]
    times = [owned_times(devices, freqs, p) for p in range(CHUNKS)]
    moved = []
    for p in range(CHUNKS):
        tau = pl.pallas_call(
            to_time_kernel,
            out_shape=jax.ShapeDtypeStruct((devices, 2, entries, slots, points), f32),
            in_specs=[VMEM] * 5,
            out_specs=VMEM,
            compiler_params=PARAMS,
            cost_estimate=pl.CostEstimate(flops=6 * 10**9 // CHUNKS, bytes_accessed=8 * 2**20, transcendentals=0),
        )(green, *time_tables(times[p], freqs))
        moved.append(lax.all_to_all(tau, "kb", 0, 0, tiled=True))
    arrived = []
    for p in range(CHUNKS):
        chi = pl.pallas_call(
            bubble_kernel,
            out_shape=jax.ShapeDtypeStruct((devices, 2, comps, slots, points), f32),
            in_specs=[SMEM, SMEM] + [VMEM] * 7,
            out_specs=VMEM,
            scratch_shapes=[
                pltpu.VMEM((side, entries, slots, 2 * plane), f32),
                pltpu.VMEM((side, entries, slots, 2 * plane), f32),
                pltpu.VMEM((side, entries, slots, 2 * plane), f32),
                pltpu.VMEM((comps, side, slots, 2 * plane), f32),
            ],
            compiler_params=PARAMS,
            cost_estimate=pl.CostEstimate(flops=12 * 10**9 // CHUNKS, bytes_accessed=16 * 2**20, transcendentals=0),
        )(pair_table, mirror_map, moved[p], *ahead, *mirrored, *inverse)
        arrived.append(lax.all_to_all(chi, "kb", 0, 0, tiled=True))
    out = None
    block = comps // 2
    for p in range(CHUNKS):
        table = pl.BlockSpec((2 * freqs // CHUNKS, 2 * freqs), lambda i: (0, 0))
        result = pl.BlockSpec((2, block, points, freqs), lambda i: (0, i, 0, 0))
        out = pl.pallas_call(
            functools.partial(to_frequency_kernel, out is None),
            grid=(comps // block,),
            out_shape=jax.ShapeDtypeStruct((2, comps, points, freqs), f32),
            in_specs=[pl.BlockSpec((devices, 2, block, slots, points), lambda i: (0, 0, i, 0, 0)), table, table]
            + ([] if out is None else [result]),
            out_specs=result,
            input_output_aliases={} if out is None else {3: 0},
            compiler_params=PARAMS,
            cost_estimate=pl.CostEstimate(flops=12 * 10**9 // CHUNKS, bytes_accessed=16 * 2**20, transcendentals=0),
        )(arrived[p], *frequency_tables(times[p], freqs), *([] if out is None else [out]))
    return out


def solution(mesh):
    placed = (P("set", None, "kb", None), P(), P("set", None))
    return jax.shard_map(
        functools.partial(local, mesh.shape["kb"]),
        mesh=mesh,
        in_specs=placed,
        out_specs=P("set", None, "kb", None),
        check_vma=False,
    )
```

```python
import functools

import numpy as np
import ml_dtypes
import jax
import jax.numpy as jnp
from jax import lax
from jax.experimental import pallas as pl
from jax.experimental.pallas import tpu as pltpu
from jax.sharding import PartitionSpec as P

CHUNKS = 2
VMEM = pl.BlockSpec(memory_space=pltpu.VMEM)
SMEM = pl.BlockSpec(memory_space=pltpu.SMEM)
PARAMS = pltpu.CompilerParams(vmem_limit_bytes=48 * 1024 * 1024)


def split_np(table):
    table = table.astype(np.float32)
    high = table.astype(ml_dtypes.bfloat16)
    low = (table - high.astype(np.float32)).astype(ml_dtypes.bfloat16)
    return high, low


def split(x):
    high = x.astype(jnp.bfloat16)
    return high, (x - high.astype(jnp.float32)).astype(jnp.bfloat16)


def mm(a, b, dims):
    return lax.dot_general(a, b, (dims, ((), ())), preferred_element_type=jnp.float32)


def mm3(a, b, dims=((1,), (0,))):
    return mm(a[0], b[0], dims) + mm(a[1], b[0], dims) + mm(a[0], b[1], dims)


def owned_times(devices, freqs, chunk):
    per = freqs // (2 * CHUNKS * devices)
    first = chunk * (freqs // (2 * CHUNKS)) + np.arange(devices)[:, None] * per + np.arange(per)[None, :]
    return np.stack([first, freqs - 1 - first], axis=1).reshape(-1)


def time_tables(times, freqs):
    angle = ((2 * np.arange(freqs)[None, :] - freqs + 1) * (2 * times[:, None] + 1)) % (4 * freqs)
    angle = angle * (2 * np.pi / (4 * freqs))
    scale = freqs**-0.5
    return split_np(scale * np.cos(angle)) + split_np(scale * np.sin(angle))


def frequency_tables(times, freqs):
    angle = ((np.arange(freqs)[None, :] - freqs // 2) * (2 * times[:, None] + 1)) % (2 * freqs)
    angle = angle * (2 * np.pi / (2 * freqs))
    cos, sin = np.cos(angle) * freqs**-0.5, np.sin(angle) * freqs**-0.5
    return split_np(np.block([[cos, sin], [-sin, cos]]))


def plane_table(side, sign):
    index = np.arange(side * side)
    upper, lower = index // side, index % side
    angle = (upper[:, None] * upper[None, :] + lower[:, None] * lower[None, :]) % side * (2 * np.pi / side)
    scale = (side**3) ** -0.5
    cos, sin = scale * np.cos(angle), sign * scale * np.sin(angle)
    return split_np(np.block([[cos, sin], [-sin, cos]]))


def cadd(a, b):
    return a[0] + b[0], a[1] + b[1]


def csub(a, b):
    return a[0] - b[0], a[1] - b[1]


def dft4(a, sign):
    s02, d02 = cadd(a[0], a[2]), csub(a[0], a[2])
    s13, d13 = cadd(a[1], a[3]), csub(a[1], a[3])
    turned = (-d13[1], d13[0]) if sign > 0 else (d13[1], -d13[0])
    return [cadd(s02, s13), cadd(d02, turned), csub(s02, s13), csub(d02, turned)]


def twiddle(a, power, sign):
    if power == 0:
        return a
    if power == 4:
        return (-a[1], a[0]) if sign > 0 else (a[1], -a[0])
    if power in (2, 6):
        r = np.float32(np.sqrt(0.5))
        plus, minus = (a[0] + a[1]) * r, (a[0] - a[1]) * r
        if power == 2:
            return (minus, plus) if sign > 0 else (plus, -minus)
        return (-plus, minus) if sign > 0 else (-minus, -plus)
    c = np.float32(np.cos(2 * np.pi * power / 16))
    s = np.float32(sign * np.sin(2 * np.pi * power / 16))
    return a[0] * c - a[1] * s, a[0] * s + a[1] * c


def dft16(x, sign):
    columns = [dft4([x[4 * n1 + n2] for n1 in range(4)], sign) for n2 in range(4)]
    out = [None] * 16
    for k1 in range(4):
        row = dft4([twiddle(columns[n2][k1], n2 * k1, sign) for n2 in range(4)], sign)
        for k2 in range(4):
            out[k1 + 4 * k2] = row[k2]
    return out


def to_time(g_ref, table, o_ref, p):
    devices, _, entries, slots, points = o_ref.shape[1:]
    freqs = g_ref.shape[-1]
    cos, sin = (table[p, 0], table[p, 1]), (table[p, 2], table[p, 3])
    dims = ((1,), (1,))
    re = split(g_ref[0].reshape(entries * points, freqs))
    im = split(g_ref[1].reshape(entries * points, freqs))
    tau = (mm3(cos, re, dims) + mm3(sin, im, dims), mm3(cos, im, dims) - mm3(sin, re, dims))
    for part in range(2):
        for e in range(entries):
            o_ref[p, :, part, e] = tau[part][:, e * points:(e + 1) * points].reshape(devices, slots, points)


def bubble(pair_ref, mirror_ref, x_ref, ahead, mirrored, inverse, o_ref, y, g, gm, chi, p):
    devices, _, entries, slots, points = x_ref.shape[1:]
    side = y.shape[0]
    plane = side * side
    halves = devices // side
    comps = o_ref.shape[3]

    def forth(e, carry):
        for h in range(halves):
            cells = [(x_ref[p, k * halves + h, 0, e], x_ref[p, k * halves + h, 1, e]) for k in range(side)]
            for k, (re, im) in enumerate(dft16(cells, 1)):
                y[k, e, :, h * points:(h + 1) * points] = re
                y[k, e, :, plane + h * points:plane + (h + 1) * points] = im
        return carry

    lax.fori_loop(0, entries, forth, 0)
    rows = split(y[...].reshape(side * entries * slots, 2 * plane))
    g[...] = mm3(rows, (ahead[0], ahead[1])).reshape(g.shape)
    other = mm3(rows, (mirrored[0], mirrored[1])).reshape(side * entries, slots, 2 * plane)
    other = jnp.concatenate([other[:, slots // 2:], other[:, :slots // 2]], axis=1)
    gm[...] = other.reshape(gm.shape)

    def one(c, carry):
        left, right = pair_ref[c, 0], pair_ref[c, 1]
        for r in range(side):
            a = g[r, left]
            b = gm[mirror_ref[0, r], right]
            ar, ai, br, bi = a[:, :plane], a[:, plane:], b[:, :plane], b[:, plane:]
            chi[c, r, :, :plane] = ar * br - ai * bi
            chi[c, r, :, plane:] = ar * bi + ai * br
        return carry

    lax.fori_loop(0, comps, one, 0)
    rows = split(chi[...].reshape(comps * side * slots, 2 * plane))
    chi[...] = mm3(rows, (inverse[0], inverse[1])).reshape(chi.shape)

    def back(c, carry):
        for h in range(halves):
            lanes = slice(h * points, (h + 1) * points)
            high = slice(plane + h * points, plane + (h + 1) * points)
            cells = [(chi[c, r, :, lanes], chi[c, r, :, high]) for r in range(side)]
            for q, (re, im) in enumerate(dft16(cells, -1)):
                o_ref[p, q * halves + h, 0, c] = re
                o_ref[p, q * halves + h, 1, c] = im
        return carry

    lax.fori_loop(0, comps, back, 0)


def main_kernel(pair_ref, mirror_ref, g_hbm, time_hbm, plane_hbm, o_hbm,
                green, table, planes, mirrored, tau, x, y, g, gm, chi, sent,
                load, own, send, recv):
    devices = tau.shape[1]
    side = y.shape[0]
    plane = side * side
    me = lax.axis_index("kb")
    loads = [pltpu.make_async_copy(src, dst, load.at[i])
             for i, (src, dst) in enumerate([(g_hbm, green), (time_hbm, table), (plane_hbm, planes)])]
    for copy in loads:
        copy.start()
    barrier = pltpu.get_barrier_semaphore()

    def greet(s, carry):
        pl.semaphore_signal(barrier, inc=1, device_id={"kb": lax.rem(me + s, devices)},
                            device_id_type=pl.DeviceIdType.MESH)
        return carry

    lax.fori_loop(1, devices, greet, 0)

    def exchange(src, dst, p, n):
        pltpu.make_async_copy(src.at[p, me], dst.at[p, me], own.at[n]).start()

        def one(i, carry):
            step = (i + 1) // 2
            shift = devices // 2 + step * (2 * lax.rem(i, 2) - 1)
            pltpu.make_async_remote_copy(
                src_ref=src.at[p, me_plus(shift)], dst_ref=dst.at[p, me],
                send_sem=send.at[n], recv_sem=recv.at[n],
                device_id={"kb": me_plus(shift)}, device_id_type=pl.DeviceIdType.MESH,
            ).start()
            return carry

        lax.fori_loop(0, devices - 1, one, 0)

    def me_plus(shift):
        return lax.rem(me + shift, devices)

    def finish(ref, p, sem):
        part = ref.at[p, pl.ds(0, devices - 1)]
        pltpu.make_async_copy(part, part, sem).wait()

    loads[0].wait()
    loads[1].wait()
    for p in range(CHUNKS):
        to_time(green, table, tau, p)
        if p == 0:
            pl.semaphore_wait(barrier, devices - 1)
        exchange(tau, x, p, p)
    loads[2].wait()
    lane = lax.broadcasted_iota(jnp.int32, (plane, plane), 1)
    ry, rz = lane // side, lane % side
    target = (mirror_ref[1, 0] + side - ry) % side * side + (mirror_ref[2, 0] + side - rz) % side
    pick = (lax.broadcasted_iota(jnp.int32, (plane, plane), 0) == target).astype(jnp.float32).astype(jnp.bfloat16)
    for i in range(2):
        for part in range(2):
            lanes = slice(part * plane, (part + 1) * plane)
            mirrored[i, :, lanes] = mm(planes[i, :, lanes], pick, ((1,), (0,))).astype(jnp.bfloat16)
    for p in range(CHUNKS):
        n = CHUNKS + p
        pltpu.make_async_copy(tau.at[p, me], x.at[p, me], own.at[p]).wait()
        finish(x, p, recv.at[p])
        bubble(pair_ref, mirror_ref, x, planes.at[0:2], mirrored, planes.at[2:4], sent, y, g, gm, chi, p)
        exchange(sent, o_hbm, p, n)
    for p in range(CHUNKS):
        n = CHUNKS + p
        finish(tau, p, send.at[p])
        pltpu.make_async_copy(sent.at[p, me], o_hbm.at[p, me], own.at[n]).wait()
        finish(sent, p, send.at[n])
        finish(o_hbm, p, recv.at[n])


def to_frequency_kernel(x_ref, b_ref, o_ref):
    _, devices, _, block, slots, points = x_ref.shape
    freqs = o_ref.shape[-1]
    rows = []
    for c in range(block):
        parts = [x_ref[p, :, part, c].reshape(devices * slots, points).T
                 for p in range(CHUNKS) for part in range(2)]
        rows.append(jnp.concatenate(parts, axis=1))
    value = mm3(split(jnp.concatenate(rows, axis=0)), (b_ref[0], b_ref[1]))
    for part in range(2):
        o_ref[part] = value[:, part * freqs:(part + 1) * freqs].reshape(block, points, freqs)


def local(devices, green, pair_table, mirror_map):
    entries, points, freqs = green.shape[1:]
    side = mirror_map.shape[1]
    plane = side * side
    comps = pair_table.shape[0]
    slots = freqs // (devices * CHUNKS)
    f32, bf16 = jnp.float32, jnp.bfloat16
    times = [owned_times(devices, freqs, p) for p in range(CHUNKS)]
    time_table = np.stack([np.stack(time_tables(t, freqs)) for t in times])
    plane_tables = np.stack(plane_table(side, 1.0) + plane_table(side, -1.0))
    back = [frequency_tables(t, freqs) for t in times]
    frequency_table = np.stack([np.concatenate([b[i] for b in back], axis=0) for i in range(2)])
    hbm = pl.BlockSpec(memory_space=pl.ANY)
    cells = (side, entries, slots, 2 * plane)
    arrived = pl.pallas_call(
        main_kernel,
        out_shape=jax.ShapeDtypeStruct((CHUNKS, devices, 2, comps, slots, points), f32),
        in_specs=[SMEM, SMEM, hbm, hbm, hbm],
        out_specs=hbm,
        scratch_shapes=[
            pltpu.VMEM(green.shape, f32),
            pltpu.VMEM(time_table.shape, bf16),
            pltpu.VMEM(plane_tables.shape, bf16),
            pltpu.VMEM((2, 2 * plane, 2 * plane), bf16),
            pltpu.VMEM((CHUNKS, devices, 2, entries, slots, points), f32),
            pltpu.VMEM((CHUNKS, devices, 2, entries, slots, points), f32),
            pltpu.VMEM(cells, f32),
            pltpu.VMEM(cells, f32),
            pltpu.VMEM(cells, f32),
            pltpu.VMEM((comps,) + (side, slots, 2 * plane), f32),
            pltpu.VMEM((CHUNKS, devices, 2, comps, slots, points), f32),
            pltpu.SemaphoreType.DMA((3,)),
            pltpu.SemaphoreType.DMA((2 * CHUNKS,)),
            pltpu.SemaphoreType.DMA((2 * CHUNKS,)),
            pltpu.SemaphoreType.DMA((2 * CHUNKS,)),
        ],
        compiler_params=pltpu.CompilerParams(
            vmem_limit_bytes=56 * 1024 * 1024, collective_id=0, has_side_effects=True
        ),
        cost_estimate=pl.CostEstimate(flops=18 * 10**9, bytes_accessed=16 * 2**20, transcendentals=0),
    )(pair_table, mirror_map, green, time_table, plane_tables)
    block = comps // 2
    return pl.pallas_call(
        to_frequency_kernel,
        grid=(comps // block,),
        out_shape=jax.ShapeDtypeStruct((2, comps, points, freqs), f32),
        in_specs=[
            pl.BlockSpec((CHUNKS, devices, 2, block, slots, points), lambda i: (0, 0, 0, i, 0, 0)),
            pl.BlockSpec((2, 2 * freqs, 2 * freqs), lambda i: (0, 0, 0)),
        ],
        out_specs=pl.BlockSpec((2, block, points, freqs), lambda i: (0, i, 0, 0)),
        compiler_params=PARAMS,
        cost_estimate=pl.CostEstimate(flops=12 * 10**9, bytes_accessed=16 * 2**20, transcendentals=0),
    )(arrived, frequency_table)


def solution(mesh):
    placed = (P("set", None, "kb", None), P(), P("set", None))
    return jax.shard_map(
        functools.partial(local, mesh.shape["kb"]),
        mesh=mesh,
        in_specs=placed,
        out_specs=P("set", None, "kb", None),
        check_vma=False,
    )
```

```python
import functools

import numpy as np
import ml_dtypes
import jax
import jax.numpy as jnp
from jax import lax
from jax.experimental import pallas as pl
from jax.experimental.pallas import tpu as pltpu
from jax.sharding import PartitionSpec as P

CHUNKS = 2
SMEM = pl.BlockSpec(memory_space=pltpu.SMEM)


def split_np(table):
    table = table.astype(np.float32)
    high = table.astype(ml_dtypes.bfloat16)
    low = (table - high.astype(np.float32)).astype(ml_dtypes.bfloat16)
    return high, low


def split(x):
    high = x.astype(jnp.bfloat16)
    return high, (x - high.astype(jnp.float32)).astype(jnp.bfloat16)


def mm(a, b, dims):
    return lax.dot_general(a, b, (dims, ((), ())), preferred_element_type=jnp.float32)


def mm3(a, b, dims=((1,), (0,))):
    return mm(a[0], b[0], dims) + mm(a[1], b[0], dims) + mm(a[0], b[1], dims)


def owned_times(devices, freqs, chunk):
    per = freqs // (2 * CHUNKS * devices)
    first = chunk * (freqs // (2 * CHUNKS)) + np.arange(devices)[:, None] * per + np.arange(per)[None, :]
    return np.stack([first, freqs - 1 - first], axis=1).reshape(-1)


def time_tables(times, freqs):
    angle = ((2 * np.arange(freqs)[None, :] - freqs + 1) * (2 * times[:, None] + 1)) % (4 * freqs)
    angle = angle * (2 * np.pi / (4 * freqs))
    scale = freqs**-0.5
    return split_np(scale * np.cos(angle)) + split_np(scale * np.sin(angle))


def frequency_tables(times, freqs):
    angle = ((np.arange(freqs)[None, :] - freqs // 2) * (2 * times[:, None] + 1)) % (2 * freqs)
    angle = angle * (2 * np.pi / (2 * freqs))
    cos, sin = np.cos(angle) * freqs**-0.5, np.sin(angle) * freqs**-0.5
    return split_np(np.block([[cos, sin], [-sin, cos]]))


def plane_table(side, sign):
    index = np.arange(side * side)
    upper, lower = index // side, index % side
    angle = (upper[:, None] * upper[None, :] + lower[:, None] * lower[None, :]) % side * (2 * np.pi / side)
    scale = (side**3) ** -0.5
    cos, sin = scale * np.cos(angle), sign * scale * np.sin(angle)
    return split_np(np.block([[cos, sin], [-sin, cos]]))


def cadd(a, b):
    return a[0] + b[0], a[1] + b[1]


def csub(a, b):
    return a[0] - b[0], a[1] - b[1]


def dft4(a, sign):
    s02, d02 = cadd(a[0], a[2]), csub(a[0], a[2])
    s13, d13 = cadd(a[1], a[3]), csub(a[1], a[3])
    turned = (-d13[1], d13[0]) if sign > 0 else (d13[1], -d13[0])
    return [cadd(s02, s13), cadd(d02, turned), csub(s02, s13), csub(d02, turned)]


def twiddle(a, power, sign):
    if power == 0:
        return a
    if power == 4:
        return (-a[1], a[0]) if sign > 0 else (a[1], -a[0])
    if power in (2, 6):
        r = np.float32(np.sqrt(0.5))
        plus, minus = (a[0] + a[1]) * r, (a[0] - a[1]) * r
        if power == 2:
            return (minus, plus) if sign > 0 else (plus, -minus)
        return (-plus, minus) if sign > 0 else (-minus, -plus)
    c = np.float32(np.cos(2 * np.pi * power / 16))
    s = np.float32(sign * np.sin(2 * np.pi * power / 16))
    return a[0] * c - a[1] * s, a[0] * s + a[1] * c


def dft16(x, sign):
    columns = [dft4([x[4 * n1 + n2] for n1 in range(4)], sign) for n2 in range(4)]
    out = [None] * 16
    for k1 in range(4):
        row = dft4([twiddle(columns[n2][k1], n2 * k1, sign) for n2 in range(4)], sign)
        for k2 in range(4):
            out[k1 + 4 * k2] = row[k2]
    return out


def to_time(g_ref, table, o_ref, p):
    devices, _, entries, slots, points = o_ref.shape[1:]
    freqs = g_ref.shape[-1]
    cos, sin = (table[p, 0], table[p, 1]), (table[p, 2], table[p, 3])
    dims = ((1,), (1,))
    re = split(g_ref[0].reshape(entries * points, freqs))
    im = split(g_ref[1].reshape(entries * points, freqs))
    tau = (mm3(cos, re, dims) + mm3(sin, im, dims), mm3(cos, im, dims) - mm3(sin, re, dims))
    for part in range(2):
        for e in range(entries):
            o_ref[p, :, part, e] = tau[part][:, e * points:(e + 1) * points].reshape(devices, slots, points)


def bubble(pair_ref, mirror_ref, x_ref, ahead, mirrored, inverse, o_ref, y, g, gm, chi, p):
    devices, _, entries, slots, points = x_ref.shape[1:]
    side = y.shape[0]
    plane = side * side
    halves = devices // side
    comps = o_ref.shape[3]

    def forth(e, carry):
        for h in range(halves):
            cells = [(x_ref[p, k * halves + h, 0, e], x_ref[p, k * halves + h, 1, e]) for k in range(side)]
            for k, (re, im) in enumerate(dft16(cells, 1)):
                y[k, e, :, h * points:(h + 1) * points] = re
                y[k, e, :, plane + h * points:plane + (h + 1) * points] = im
        return carry

    lax.fori_loop(0, entries, forth, 0)
    rows = split(y[...].reshape(side * entries * slots, 2 * plane))
    g[...] = mm3(rows, (ahead[0], ahead[1])).reshape(g.shape)
    other = mm3(rows, (mirrored[0], mirrored[1])).reshape(side * entries, slots, 2 * plane)
    other = jnp.concatenate([other[:, slots // 2:], other[:, :slots // 2]], axis=1)
    gm[...] = other.reshape(gm.shape)

    def one(c, carry):
        left, right = pair_ref[0, c], pair_ref[1, c]
        for r in range(side):
            a = g[r, left]
            b = gm[mirror_ref[0, r], right]
            ar, ai, br, bi = a[:, :plane], a[:, plane:], b[:, :plane], b[:, plane:]
            chi[c, r, :, :plane] = ar * br - ai * bi
            chi[c, r, :, plane:] = ar * bi + ai * br
        return carry

    lax.fori_loop(0, comps, one, 0)
    rows = split(chi[...].reshape(comps * side * slots, 2 * plane))
    chi[...] = mm3(rows, (inverse[0], inverse[1])).reshape(chi.shape)

    def back(c, carry):
        for h in range(halves):
            lanes = slice(h * points, (h + 1) * points)
            high = slice(plane + h * points, plane + (h + 1) * points)
            cells = [(chi[c, r, :, lanes], chi[c, r, :, high]) for r in range(side)]
            for q, (re, im) in enumerate(dft16(cells, -1)):
                o_ref[p, q * halves + h, 0, c] = re
                o_ref[p, q * halves + h, 1, c] = im
        return carry

    lax.fori_loop(0, comps, back, 0)


def main_kernel(pair_ref, mirror_ref, green, time_hbm, plane_hbm, back_hbm, half_hbm, last,
                table, planes, back, mirrored, tau, x, y, g, gm, chi, sent, got, acc,
                load, own, send, recv):
    devices = tau.shape[1]
    side = y.shape[0]
    plane = side * side
    me = lax.axis_index("kb")
    loads = [pltpu.make_async_copy(src, dst, load.at[i])
             for i, (src, dst) in enumerate([(time_hbm, table), (plane_hbm, planes), (back_hbm, back)])]
    for copy in loads:
        copy.start()
    barrier = pltpu.get_barrier_semaphore()

    def greet(s, carry):
        pl.semaphore_signal(barrier, inc=1, device_id={"kb": lax.rem(me + s, devices)},
                            device_id_type=pl.DeviceIdType.MESH)
        return carry

    lax.fori_loop(1, devices, greet, 0)

    def partner(shift):
        total, bit = 0, 1
        while bit < devices:
            total += bit * lax.rem(me // bit + shift // bit, 2)
            bit *= 2
        return total

    def exchange(src, dst, n):
        pltpu.make_async_copy(src.at[me], dst.at[me], own.at[n]).start()

        def one(i, carry):
            other = partner(i // 4 + devices // 4 * lax.rem(i + 2, 4))
            pltpu.make_async_remote_copy(
                src_ref=src.at[other], dst_ref=dst.at[me], send_sem=send.at[n], recv_sem=recv.at[n],
                device_id={"kb": other}, device_id_type=pl.DeviceIdType.MESH,
            ).start()
            return carry

        lax.fori_loop(0, 2, one, 0)
        lax.fori_loop(3, devices, one, 0)

    def finish(ref, sem):
        part = ref.at[pl.ds(0, devices - 1)]
        pltpu.make_async_copy(part, part, sem).wait()

    loads[0].wait()
    for p in range(CHUNKS):
        to_time(green, table, tau, p)
        if p == 0:
            pl.semaphore_wait(barrier, devices - 1)
        exchange(tau.at[p], x.at[p], p)
    loads[1].wait()
    lane = lax.broadcasted_iota(jnp.int32, (plane, plane), 1)
    ry, rz = lane // side, lane % side
    target = (mirror_ref[1, 0] + side - ry) % side * side + (mirror_ref[2, 0] + side - rz) % side
    pick = (lax.broadcasted_iota(jnp.int32, (plane, plane), 0) == target).astype(jnp.float32).astype(jnp.bfloat16)
    for i in range(2):
        for part in range(2):
            lanes = slice(part * plane, (part + 1) * plane)
            mirrored[i, :, lanes] = mm(planes[i, :, lanes], pick, ((1,), (0,))).astype(jnp.bfloat16)
    landing = [got, last]
    for p in range(CHUNKS):
        pltpu.make_async_copy(tau.at[p, me], x.at[p, me], own.at[p]).wait()
        finish(x.at[p], recv.at[p])
        bubble(pair_ref, mirror_ref, x, planes.at[0:2], mirrored, planes.at[2:4], sent, y, g, gm, chi, p)
        exchange(sent.at[p], landing[p], CHUNKS + p)
    pltpu.make_async_copy(sent.at[0, me], got.at[me], own.at[CHUNKS]).wait()
    finish(got, recv.at[CHUNKS])
    loads[2].wait()
    comps = got.shape[2]
    block = comps // 2
    for i in range(2):
        chosen = slice(i * block, (i + 1) * block)
        value = to_frequency(got.at[:, :, chosen], back)
        for part in range(2):
            acc[part, chosen] = value[part]
    store = pltpu.make_async_copy(acc, half_hbm, load.at[3])
    store.start()
    for p in range(CHUNKS):
        finish(tau.at[p], send.at[p])
        finish(sent.at[p], send.at[CHUNKS + p])
    store.wait()
    pltpu.make_async_copy(sent.at[1, me], last.at[me], own.at[CHUNKS + 1]).wait()
    finish(last, recv.at[CHUNKS + 1])


def to_frequency(x_ref, b_ref):
    devices, _, block, slots, points = x_ref.shape
    freqs = b_ref.shape[-1] // 2
    rows = []
    for c in range(block):
        parts = [x_ref[:, part, c].reshape(devices * slots, points).T for part in range(2)]
        rows.append(jnp.concatenate(parts, axis=1))
    value = mm3(split(jnp.concatenate(rows, axis=0)), (b_ref[0], b_ref[1]))
    return [value[:, part * freqs:(part + 1) * freqs].reshape(block, points, freqs) for part in range(2)]


def finish_kernel(x_ref, b_ref, half_ref, o_ref):
    value = to_frequency(x_ref, b_ref)
    for part in range(2):
        o_ref[part] = half_ref[part] + value[part]


def local(devices, green, pair_table, mirror_map):
    entries, points, freqs = green.shape[1:]
    side = mirror_map.shape[1]
    plane = side * side
    comps = pair_table.shape[0]
    slots = freqs // (devices * CHUNKS)
    f32, bf16 = jnp.float32, jnp.bfloat16
    times = [owned_times(devices, freqs, p) for p in range(CHUNKS)]
    time_table = np.stack([np.stack(time_tables(t, freqs)) for t in times])
    plane_tables = np.stack(plane_table(side, 1.0) + plane_table(side, -1.0))
    frequency_table = [np.stack(frequency_tables(t, freqs)) for t in times]
    hbm = pl.BlockSpec(memory_space=pl.ANY)
    cells = (side, entries, slots, 2 * plane)
    exchanged = (devices, 2, comps, slots, points)
    result = (2, comps, points, freqs)
    half, last = pl.pallas_call(
        main_kernel,
        out_shape=[jax.ShapeDtypeStruct(result, f32), jax.ShapeDtypeStruct(exchanged, f32)],
        in_specs=[SMEM, SMEM, pl.BlockSpec(memory_space=pltpu.VMEM), hbm, hbm, hbm],
        out_specs=[hbm, hbm],
        scratch_shapes=[
            pltpu.VMEM(time_table.shape, bf16),
            pltpu.VMEM(plane_tables.shape, bf16),
            pltpu.VMEM(frequency_table[0].shape, bf16),
            pltpu.VMEM((2, 2 * plane, 2 * plane), bf16),
            pltpu.VMEM((CHUNKS, devices, 2, entries, slots, points), f32),
            pltpu.VMEM((CHUNKS, devices, 2, entries, slots, points), f32),
            pltpu.VMEM(cells, f32),
            pltpu.VMEM(cells, f32),
            pltpu.VMEM(cells, f32),
            pltpu.VMEM((comps,) + (side, slots, 2 * plane), f32),
            pltpu.VMEM((CHUNKS,) + exchanged, f32),
            pltpu.VMEM(exchanged, f32),
            pltpu.VMEM(result, f32),
            pltpu.SemaphoreType.DMA((4,)),
            pltpu.SemaphoreType.DMA((2 * CHUNKS,)),
            pltpu.SemaphoreType.DMA((2 * CHUNKS,)),
            pltpu.SemaphoreType.DMA((2 * CHUNKS,)),
        ],
        compiler_params=pltpu.CompilerParams(
            vmem_limit_bytes=48 * 1024 * 1024, collective_id=0, has_side_effects=True
        ),
        cost_estimate=pl.CostEstimate(flops=18 * 10**9, bytes_accessed=16 * 2**20, transcendentals=0),
    )(pair_table.T, mirror_map, green, time_table, plane_tables, frequency_table[0])
    block = comps // 4
    whole = pl.BlockSpec((2, block, points, freqs), lambda i: (0, i, 0, 0))
    return pl.pallas_call(
        finish_kernel,
        grid=(comps // block,),
        out_shape=jax.ShapeDtypeStruct(result, f32),
        in_specs=[
            pl.BlockSpec((devices, 2, block, slots, points), lambda i: (0, 0, i, 0, 0)),
            pl.BlockSpec(frequency_table[1].shape, lambda i: (0, 0, 0)),
            whole,
        ],
        out_specs=whole,
        compiler_params=pltpu.CompilerParams(vmem_limit_bytes=58 * 1024 * 1024),
        cost_estimate=pl.CostEstimate(flops=6 * 10**9, bytes_accessed=16 * 2**20, transcendentals=0),
    )(last, frequency_table[1], half)


def solution(mesh):
    placed = (P("set", None, "kb", None), P(), P("set", None))
    return jax.shard_map(
        functools.partial(local, mesh.shape["kb"]),
        mesh=mesh,
        in_specs=placed,
        out_specs=P("set", None, "kb", None),
        check_vma=False,
    )
```

```python
import functools

import numpy as np
import ml_dtypes
import jax
import jax.numpy as jnp
from jax import lax
from jax.experimental import pallas as pl
from jax.experimental.pallas import tpu as pltpu
from jax.sharding import PartitionSpec as P

CHUNKS = 2
SMEM = pl.BlockSpec(memory_space=pltpu.SMEM)


def split_np(table):
    table = table.astype(np.float32)
    high = table.astype(ml_dtypes.bfloat16)
    low = (table - high.astype(np.float32)).astype(ml_dtypes.bfloat16)
    return high, low


def split(x):
    high = x.astype(jnp.bfloat16)
    return high, (x - high.astype(jnp.float32)).astype(jnp.bfloat16)


def mm(a, b, dims):
    return lax.dot_general(a, b, (dims, ((), ())), preferred_element_type=jnp.float32)


def mm3(a, b, dims=((1,), (0,))):
    return mm(a[0], b[0], dims) + mm(a[1], b[0], dims) + mm(a[0], b[1], dims)


def owned_times(devices, freqs, chunk):
    per = freqs // (2 * CHUNKS * devices)
    first = chunk * (freqs // (2 * CHUNKS)) + np.arange(devices)[:, None] * per + np.arange(per)[None, :]
    return np.stack([first, freqs - 1 - first], axis=1).reshape(-1)


def time_tables(times, freqs):
    angle = ((2 * np.arange(freqs)[None, :] - freqs + 1) * (2 * times[:, None] + 1)) % (4 * freqs)
    angle = angle * (2 * np.pi / (4 * freqs))
    scale = freqs**-0.5
    return split_np(scale * np.cos(angle)) + split_np(scale * np.sin(angle))


def frequency_tables(times, freqs):
    angle = ((np.arange(freqs)[None, :] - freqs // 2) * (2 * times[:, None] + 1)) % (2 * freqs)
    angle = angle * (2 * np.pi / (2 * freqs))
    cos, sin = np.cos(angle) * freqs**-0.5, np.sin(angle) * freqs**-0.5
    return split_np(np.block([[cos, sin], [-sin, cos]]))


def plane_table(side, sign):
    index = np.arange(side * side)
    upper, lower = index // side, index % side
    angle = (upper[:, None] * upper[None, :] + lower[:, None] * lower[None, :]) % side * (2 * np.pi / side)
    scale = (side**3) ** -0.5
    cos, sin = scale * np.cos(angle), sign * scale * np.sin(angle)
    return split_np(np.block([[cos, sin], [-sin, cos]]))


def cadd(a, b):
    return a[0] + b[0], a[1] + b[1]


def csub(a, b):
    return a[0] - b[0], a[1] - b[1]


def dft4(a, sign):
    s02, d02 = cadd(a[0], a[2]), csub(a[0], a[2])
    s13, d13 = cadd(a[1], a[3]), csub(a[1], a[3])
    turned = (-d13[1], d13[0]) if sign > 0 else (d13[1], -d13[0])
    return [cadd(s02, s13), cadd(d02, turned), csub(s02, s13), csub(d02, turned)]


def twiddle(a, power, sign):
    if power == 0:
        return a
    if power == 4:
        return (-a[1], a[0]) if sign > 0 else (a[1], -a[0])
    if power in (2, 6):
        r = np.float32(np.sqrt(0.5))
        plus, minus = (a[0] + a[1]) * r, (a[0] - a[1]) * r
        if power == 2:
            return (minus, plus) if sign > 0 else (plus, -minus)
        return (-plus, minus) if sign > 0 else (-minus, -plus)
    c = np.float32(np.cos(2 * np.pi * power / 16))
    s = np.float32(sign * np.sin(2 * np.pi * power / 16))
    return a[0] * c - a[1] * s, a[0] * s + a[1] * c


def dft16(x, sign):
    columns = [dft4([x[4 * n1 + n2] for n1 in range(4)], sign) for n2 in range(4)]
    out = [None] * 16
    for k1 in range(4):
        row = dft4([twiddle(columns[n2][k1], n2 * k1, sign) for n2 in range(4)], sign)
        for k2 in range(4):
            out[k1 + 4 * k2] = row[k2]
    return out


def to_time(g_ref, table, o_ref, p):
    devices, _, entries, slots, points = o_ref.shape[1:]
    freqs = g_ref.shape[-1]
    cos, sin = (table[p, 0], table[p, 1]), (table[p, 2], table[p, 3])
    dims = ((1,), (1,))
    re = split(g_ref[0].reshape(entries * points, freqs))
    im = split(g_ref[1].reshape(entries * points, freqs))
    tau = (mm3(cos, re, dims) + mm3(sin, im, dims), mm3(cos, im, dims) - mm3(sin, re, dims))
    for part in range(2):
        for e in range(entries):
            o_ref[p, :, part, e] = tau[part][:, e * points:(e + 1) * points].reshape(devices, slots, points)


def bubble(pair_ref, mirror_ref, x_ref, ahead, mirrored, inverse, o_ref, y, g, gm, chi, p):
    devices, _, entries, slots, points = x_ref.shape[1:]
    side = y.shape[0]
    plane = side * side
    halves = devices // side
    comps = o_ref.shape[3]

    def forth(e, carry):
        for h in range(halves):
            cells = [(x_ref[p, k * halves + h, 0, e], x_ref[p, k * halves + h, 1, e]) for k in range(side)]
            for k, (re, im) in enumerate(dft16(cells, 1)):
                y[k, e, :, h * points:(h + 1) * points] = re
                y[k, e, :, plane + h * points:plane + (h + 1) * points] = im
        return carry

    lax.fori_loop(0, entries, forth, 0)
    rows = split(y[...].reshape(side * entries * slots, 2 * plane))
    g[...] = mm3(rows, (ahead[0], ahead[1])).reshape(g.shape)
    other = mm3(rows, (mirrored[0], mirrored[1])).reshape(side * entries, slots, 2 * plane)
    other = jnp.concatenate([other[:, slots // 2:], other[:, :slots // 2]], axis=1)
    gm[...] = other.reshape(gm.shape)

    def one(c, carry):
        left, right = pair_ref[0, c], pair_ref[1, c]
        for r in range(side):
            a = g[r, left]
            b = gm[mirror_ref[0, r], right]
            ar, ai, br, bi = a[:, :plane], a[:, plane:], b[:, :plane], b[:, plane:]
            chi[c, r, :, :plane] = ar * br - ai * bi
            chi[c, r, :, plane:] = ar * bi + ai * br
        return carry

    lax.fori_loop(0, comps, one, 0)
    rows = split(chi[...].reshape(comps * side * slots, 2 * plane))
    chi[...] = mm3(rows, (inverse[0], inverse[1])).reshape(chi.shape)

    def back(c, carry):
        for h in range(halves):
            lanes = slice(h * points, (h + 1) * points)
            high = slice(plane + h * points, plane + (h + 1) * points)
            cells = [(chi[c, r, :, lanes], chi[c, r, :, high]) for r in range(side)]
            for q, (re, im) in enumerate(dft16(cells, -1)):
                o_ref[p, q * halves + h, 0, c] = re
                o_ref[p, q * halves + h, 1, c] = im
        return carry

    lax.fori_loop(0, comps, back, 0)


def main_kernel(pair_ref, mirror_ref, green_hbm, time_hbm, plane_hbm, back_hbm, half_hbm, last,
                green, table, planes, back, mirrored, tau, x, y, g, gm, chi, sent, got, acc,
                load, own, send, recv):
    devices = tau.shape[1]
    side = y.shape[0]
    plane = side * side
    me = lax.axis_index("kb")
    loads = [pltpu.make_async_copy(src, dst, load.at[i])
             for i, (src, dst) in enumerate([(time_hbm, table), (plane_hbm, planes), (back_hbm, back),
                                       (green_hbm, green)])]
    for i in (3, 0, 1, 2):
        loads[i].start()
    barrier = pltpu.get_barrier_semaphore()

    def greet(s, carry):
        pl.semaphore_signal(barrier, inc=1, device_id={"kb": lax.rem(me + s, devices)},
                            device_id_type=pl.DeviceIdType.MESH)
        return carry

    lax.fori_loop(1, devices, greet, 0)

    def partner(shift):
        total, bit = 0, 1
        while bit < devices:
            total += bit * lax.rem(me // bit + shift // bit, 2)
            bit *= 2
        return total

    def exchange(src, dst, n):
        pltpu.make_async_copy(src.at[me], dst.at[me], own.at[n]).start()

        def one(i, carry):
            other = partner(i // 4 + devices // 4 * lax.rem(i + 2, 4))
            pltpu.make_async_remote_copy(
                src_ref=src.at[other], dst_ref=dst.at[me], send_sem=send.at[n], recv_sem=recv.at[n],
                device_id={"kb": other}, device_id_type=pl.DeviceIdType.MESH,
            ).start()
            return carry

        lax.fori_loop(0, 2, one, 0)
        lax.fori_loop(3, devices, one, 0)

    def finish(ref, sem):
        part = ref.at[pl.ds(0, devices - 1)]
        pltpu.make_async_copy(part, part, sem).wait()

    loads[3].wait()
    loads[0].wait()
    for p in range(CHUNKS):
        to_time(green, table, tau, p)
        if p == 0:
            pl.semaphore_wait(barrier, devices - 1)
        exchange(tau.at[p], x.at[p], p)
    loads[1].wait()
    lane = lax.broadcasted_iota(jnp.int32, (plane, plane), 1)
    ry, rz = lane // side, lane % side
    target = (mirror_ref[1, 0] + side - ry) % side * side + (mirror_ref[2, 0] + side - rz) % side
    pick = (lax.broadcasted_iota(jnp.int32, (plane, plane), 0) == target).astype(jnp.float32).astype(jnp.bfloat16)
    for i in range(2):
        for part in range(2):
            lanes = slice(part * plane, (part + 1) * plane)
            mirrored[i, :, lanes] = mm(planes[i, :, lanes], pick, ((1,), (0,))).astype(jnp.bfloat16)
    landing = [got, last]
    for p in range(CHUNKS):
        pltpu.make_async_copy(tau.at[p, me], x.at[p, me], own.at[p]).wait()
        finish(x.at[p], recv.at[p])
        bubble(pair_ref, mirror_ref, x, planes.at[0:2], mirrored, planes.at[2:4], sent, y, g, gm, chi, p)
        exchange(sent.at[p], landing[p], CHUNKS + p)
    pltpu.make_async_copy(sent.at[0, me], got.at[me], own.at[CHUNKS]).wait()
    finish(got, recv.at[CHUNKS])
    loads[2].wait()
    comps = got.shape[2]
    block = comps // 2
    for i in range(2):
        chosen = slice(i * block, (i + 1) * block)
        value = to_frequency(got.at[:, :, chosen], back)
        for part in range(2):
            acc[part, chosen] = value[part]
    store = pltpu.make_async_copy(acc, half_hbm, load.at[4])
    store.start()
    for p in range(CHUNKS):
        finish(tau.at[p], send.at[p])
        finish(sent.at[p], send.at[CHUNKS + p])
    store.wait()
    pltpu.make_async_copy(sent.at[1, me], last.at[me], own.at[CHUNKS + 1]).wait()
    finish(last, recv.at[CHUNKS + 1])


def to_frequency(x_ref, b_ref):
    devices, _, block, slots, points = x_ref.shape
    freqs = b_ref.shape[-1] // 2
    rows = []
    for c in range(block):
        parts = [x_ref[:, part, c].reshape(devices * slots, points).T for part in range(2)]
        rows.append(jnp.concatenate(parts, axis=1))
    value = mm3(split(jnp.concatenate(rows, axis=0)), (b_ref[0], b_ref[1]))
    return [value[:, part * freqs:(part + 1) * freqs].reshape(block, points, freqs) for part in range(2)]


def finish_kernel(x_ref, b_ref, half_ref, o_ref):
    value = to_frequency(x_ref, b_ref)
    for part in range(2):
        o_ref[part] = half_ref[part] + value[part]


def local(devices, green, pair_table, mirror_map):
    entries, points, freqs = green.shape[1:]
    side = mirror_map.shape[1]
    plane = side * side
    comps = pair_table.shape[0]
    slots = freqs // (devices * CHUNKS)
    f32, bf16 = jnp.float32, jnp.bfloat16
    times = [owned_times(devices, freqs, p) for p in range(CHUNKS)]
    time_table = np.stack([np.stack(time_tables(t, freqs)) for t in times])
    plane_tables = np.stack(plane_table(side, 1.0) + plane_table(side, -1.0))
    frequency_table = [np.stack(frequency_tables(t, freqs)) for t in times]
    hbm = pl.BlockSpec(memory_space=pl.ANY)
    cells = (side, entries, slots, 2 * plane)
    exchanged = (devices, 2, comps, slots, points)
    result = (2, comps, points, freqs)
    half, last = pl.pallas_call(
        main_kernel,
        out_shape=[jax.ShapeDtypeStruct(result, f32), jax.ShapeDtypeStruct(exchanged, f32)],
        in_specs=[SMEM, SMEM, hbm, hbm, hbm, hbm],
        out_specs=[hbm, hbm],
        scratch_shapes=[
            pltpu.VMEM(green.shape, f32),
            pltpu.VMEM(time_table.shape, bf16),
            pltpu.VMEM(plane_tables.shape, bf16),
            pltpu.VMEM(frequency_table[0].shape, bf16),
            pltpu.VMEM((2, 2 * plane, 2 * plane), bf16),
            pltpu.VMEM((CHUNKS, devices, 2, entries, slots, points), f32),
            pltpu.VMEM((CHUNKS, devices, 2, entries, slots, points), f32),
            pltpu.VMEM(cells, f32),
            pltpu.VMEM(cells, f32),
            pltpu.VMEM(cells, f32),
            pltpu.VMEM((comps,) + (side, slots, 2 * plane), f32),
            pltpu.VMEM((CHUNKS,) + exchanged, f32),
            pltpu.VMEM(exchanged, f32),
            pltpu.VMEM(result, f32),
            pltpu.SemaphoreType.DMA((5,)),
            pltpu.SemaphoreType.DMA((2 * CHUNKS,)),
            pltpu.SemaphoreType.DMA((2 * CHUNKS,)),
            pltpu.SemaphoreType.DMA((2 * CHUNKS,)),
        ],
        compiler_params=pltpu.CompilerParams(
            vmem_limit_bytes=60 * 1024 * 1024, collective_id=0, has_side_effects=True
        ),
        cost_estimate=pl.CostEstimate(flops=18 * 10**9, bytes_accessed=16 * 2**20, transcendentals=0),
    )(pair_table.T, mirror_map, green, time_table, plane_tables, frequency_table[0])
    block = comps // 4
    whole = pl.BlockSpec((2, block, points, freqs), lambda i: (0, i, 0, 0))
    return pl.pallas_call(
        finish_kernel,
        grid=(comps // block,),
        out_shape=jax.ShapeDtypeStruct(result, f32),
        in_specs=[
            pl.BlockSpec((devices, 2, block, slots, points), lambda i: (0, 0, i, 0, 0)),
            pl.BlockSpec(frequency_table[1].shape, lambda i: (0, 0, 0)),
            whole,
        ],
        out_specs=whole,
        compiler_params=pltpu.CompilerParams(vmem_limit_bytes=58 * 1024 * 1024),
        cost_estimate=pl.CostEstimate(flops=6 * 10**9, bytes_accessed=16 * 2**20, transcendentals=0),
    )(last, frequency_table[1], half)


def solution(mesh):
    placed = (P("set", None, "kb", None), P(), P("set", None))
    return jax.shard_map(
        functools.partial(local, mesh.shape["kb"]),
        mesh=mesh,
        in_specs=placed,
        out_specs=P("set", None, "kb", None),
        check_vma=False,
    )
```
